32 devices in a mesh: cfg: 2 (over y), row: 4 (over z), col: 2 (over x), spin: 2 (over core).
Axes of the slice: x: 2, y: 2, z: 4, core: 2. Of those that a mesh axis runs over, the one named last changes fastest.
Arguments:
- perambulator: float32 [2, 8192, 4096], P(None, ('cfg', 'row'), ('col', 'spin')), parts along dimension 1, may hold values from -1 to 1
- insertion_ops: float32 [2, 2, 64, 64], replicated, may hold values from -0.75 to 0.75
- ins_times: int32 [2], replicated, may hold values from 0 to 15
- sign_table: int32 [2, 4], replicated, may hold values from 0 to 3
- perm_table: int32 [2, 4], replicated, may hold values from 0 to 3, each once within a row
Outputs:
- generalized: float32 [2, 8192, 4096], P(None, ('cfg', 'row'), ('col', 'spin')), parts along dimension 1
The draws below stay inside these ranges and needn't reach their ends.
There are 2 independent parts, one for each index of `cfg`. The reference program is written for one: setup_inputs(seed, part) draws one part's arguments, and reference() takes and returns one part's arrays. A program takes and returns all parts, laid end to end along the dimension named above; an argument that names none is the same for every part. Nothing has to cross between parts.
All inputs are finite; a program needn't handle non-finite values.
Results may differ from the reference program's by a relative error of at most 0.0001.
Values sent between devices are 32-bit elements; how exact they have to be, the bound alone decides.
No kernel may reach another device: no remote copies, remote signals or barrier semaphores. Data moves between devices by JAX's collectives and lax.ppermute only.
A program may use at most 64 MiB of HBM per device.

```python
import jax
import jax.numpy as jnp
from jax import lax

NV = 64
NS = 4
B = 256
NT = 16
NINS = 2


def set_ends(values, own_key, least, largest):
    longest = values.shape.index(max(values.shape))
    spots = []
    for shift in (0, 1):
        where = [jax.random.randint(jax.random.fold_in(own_key, axis), (), 0, length) for axis, length in enumerate(values.shape)]
        where[longest] = (where[longest] + shift) % values.shape[longest]
        spots.append(tuple(where))
    return values.at[spots[0]].set(least).at[spots[1]].set(largest)


def block_scale(rng, shape, cuts, smallest, largest):
    gain, own = 1.0, jax.random.fold_in(rng, 6)
    for dim, blocks in cuts:
        heights = jnp.exp(jax.random.uniform(jax.random.fold_in(own, dim), (blocks,), jnp.float32, smallest / len(cuts), largest / len(cuts)))
        gain = gain * jnp.repeat(heights, shape[dim] // blocks).reshape([-1 if axis == dim else 1 for axis in range(len(shape))])
    return gain


def noise(rng, shape, spread, reach, cuts=(), held_as=jnp.bfloat16):
    gain = block_scale(rng, shape, cuts, -0.22, 0.18) if cuts else 1.0
    values = jax.random.normal(rng, shape, jnp.float32) * spread * gain
    return jnp.minimum(jnp.maximum(values, -reach), reach).astype(held_as)


def setup_inputs(seed: int = 0, part: int = 0) -> dict:
    keys = jax.random.split(jax.random.key(seed), 6)
    own_keys = jax.random.split(jax.random.fold_in(keys[5], part), 6)
    return {
        "perambulator": noise(own_keys[0], (2, NT * B, NT * B), 0.125, 1.0, ((1, 4), (2, 4)), jnp.float32),
        "insertion_ops": noise(keys[1], (NINS, 2, NV, NV), NV ** -0.5, 0.75, (), jnp.float32),
        "ins_times": jax.random.randint(keys[2], (NINS,), 0, NT).astype(jnp.int32),
        "sign_table": set_ends(jax.random.randint(keys[3], (NINS, NS), 0, 4), jax.random.fold_in(keys[3], 1), 0, 3).astype(jnp.int32),
        "perm_table": jax.vmap(lambda own: jax.random.permutation(own, NS))(jax.random.split(keys[4], NINS)).reshape((NINS, NS)).astype(jnp.int32),
    }


def complex_dot(former_real, former_imag, latter_real, latter_imag):
    maximal_precision = lax.Precision.HIGHEST
    real_part = jnp.dot(former_real, latter_real, precision=maximal_precision) - jnp.dot(former_imag, latter_imag, precision=maximal_precision)
    imag_part = jnp.dot(former_real, latter_imag, precision=maximal_precision) + jnp.dot(former_imag, latter_real, precision=maximal_precision)
    return real_part, imag_part


def insert_current_operator(row_slab, op_real, op_imag, sign_row, perm_row):
    maximal_precision = lax.Precision.HIGHEST
    col_count = row_slab.shape[2]
    slab_real = row_slab[0].reshape(NS, NV, col_count)
    slab_imag = row_slab[1].reshape(NS, NV, col_count)
    combined_real = jnp.einsum("ab,sbc->sac", op_real, slab_real, precision=maximal_precision) - jnp.einsum("ab,sbc->sac", op_imag, slab_imag, precision=maximal_precision)
    combined_imaginary = jnp.einsum("ab,sbc->sac", op_real, slab_imag, precision=maximal_precision) + jnp.einsum("ab,sbc->sac", op_imag, slab_real, precision=maximal_precision)
    selected_real = combined_real[perm_row]
    selected_imaginary = combined_imaginary[perm_row]
    phase_factor_real = jnp.array([1.0, 0.0, -1.0, 0.0], jnp.float32)[sign_row][:, None, None]
    phase_imag = jnp.array([0.0, 1.0, 0.0, -1.0], jnp.float32)[sign_row][:, None, None]
    out_real = phase_factor_real * selected_real - phase_imag * selected_imaginary
    out_imag = phase_factor_real * selected_imaginary + phase_imag * selected_real
    return out_real.reshape(B, col_count), out_imag.reshape(B, col_count)


def reference(perambulator, insertion_ops, ins_times, sign_table, perm_table):
    size_all = NT * B
    total_real = jnp.zeros((size_all, size_all), jnp.float32)
    total_imag = jnp.zeros((size_all, size_all), jnp.float32)
    for ins_index in range(NINS):
        start_row = (ins_times[ins_index] * B).astype(jnp.int32)
        row_slab = lax.dynamic_slice_in_dim(perambulator, start_row, B, 1)
        col_slab = lax.dynamic_slice_in_dim(perambulator, start_row, B, 2)
        inserted_real, inserted_imag = insert_current_operator(row_slab, insertion_ops[ins_index, 0], insertion_ops[ins_index, 1], sign_table[ins_index], perm_table[ins_index])
        part_real, part_imag = complex_dot(col_slab[0], col_slab[1], inserted_real, inserted_imag)
        total_real = total_real + part_real
        total_imag = total_imag + part_imag
    return jnp.stack([total_real, total_imag])
```

```python
import functools

import jax
import jax.numpy as jnp
from jax import lax
from jax.experimental import pallas as pl
from jax.experimental.pallas import tpu as pltpu
from jax.sharding import PartitionSpec as P

VMEM_BYTES = 40 * 1024 * 1024
LINE = 4
PIECES = 8
GROUP = 2
MINE, COLUMNS, FOLD = 1, 5, 6
BLOCKS = {7: (0,), 8: (2,), 9: (4,)}


def split(value):
    upper = value.astype(jnp.bfloat16)
    lower = (value - upper.astype(jnp.float32)).astype(jnp.bfloat16)
    return upper, lower


def three_pass(a_upper, a_lower, b_upper, b_lower):
    def dot(a, b):
        return jnp.dot(a, b, preferred_element_type=jnp.float32)

    return dot(a_upper, b_upper) + (dot(a_upper, b_lower) + dot(a_lower, b_upper))


def fold_kernel(numbers, own_ref, other_ref, op_ref, upper_ref, lower_ref, g_upper, g_lower):
    stream, half = pl.program_id(0), pl.program_id(1)
    vec_count, order = op_ref.shape[2:]
    spins = order // vec_count
    insertion = jnp.where(numbers[1] == 1, 1 - stream, stream)

    @pl.when((half == 0) & (pl.program_id(2) == 0))
    def _():
        lane_spin = lax.broadcasted_iota(jnp.int32, (vec_count, order), 1) // vec_count
        op_real, op_imag = op_ref[insertion, 0], op_ref[insertion, 1]
        for spin in range(spins):
            sign = numbers[2 + insertion * spins + spin]
            column = numbers[2 + (2 + insertion) * spins + spin]
            hit = lane_spin == column
            odd = (sign == 1) | (sign == 3)
            flip = jnp.where(sign >= 2, -1.0, 1.0)
            real = jnp.where(hit, flip * jnp.where(odd, -op_imag, op_real), 0.0)
            imag = jnp.where(hit, flip * jnp.where(odd, op_real, op_imag), 0.0)
            real_parts, imag_parts = split(real), split(imag)
            first = pl.ds(spin * vec_count, vec_count)
            second = pl.ds(order + spin * vec_count, vec_count)
            for ref, part_real, part_imag in zip((g_upper, g_lower), real_parts, imag_parts):
                ref[first, :order] = part_real
                ref[first, order:] = part_imag
                ref[second, :order] = -part_imag
                ref[second, order:] = part_real

    mine = numbers[0] == half
    joined = jnp.concatenate(
        [
            jnp.where(mine, own_ref[0, 0], other_ref[0, 0]),
            jnp.where(mine, own_ref[0, 1], other_ref[0, 1]),
        ],
        axis=1,
    )
    product = three_pass(*split(joined), g_upper[...], g_lower[...])
    upper_ref[...], lower_ref[...] = split(product)


def fold(numbers, own, other, ops):
    streams, _, rows, order = own.shape
    tile = rows // 2
    shape = jax.ShapeDtypeStruct((2 * rows, streams * 2 * order), jnp.bfloat16)
    slab_spec = pl.BlockSpec((1, 2, tile, order), lambda k, h, i, numbers: (k, 0, i, 0))
    out_spec = pl.BlockSpec((tile, 2 * order), lambda k, h, i, numbers: (2 * h + i, k))
    return pl.pallas_call(
        fold_kernel,
        grid_spec=pltpu.PrefetchScalarGridSpec(
            num_scalar_prefetch=1,
            grid=(streams, 2, 2),
            in_specs=[
                slab_spec,
                slab_spec,
                pl.BlockSpec(ops.shape, lambda k, h, i, numbers: (0, 0, 0, 0)),
            ],
            out_specs=[out_spec, out_spec],
            scratch_shapes=[pltpu.VMEM((2 * order, 2 * order), jnp.bfloat16)] * 2,
        ),
        out_shape=[shape, shape],
        compiler_params=pltpu.CompilerParams(vmem_limit_bytes=VMEM_BYTES),
        cost_estimate=pl.CostEstimate(
            flops=24 * streams * 2 * rows * order * 2 * order,
            bytes_accessed=16 * own.size,
            transcendentals=0,
        ),
        name="fold",
    )(numbers, own, other, ops)


def block_kernel(upper_ref, lower_ref, *refs):
    out_ref, r_upper, r_lower = refs[-3:]
    order = refs[0].shape[1]
    part = refs[0].shape[2]
    width = GROUP * part

    @pl.when(pl.program_id(0) == 0)
    def _():
        for index, ref in enumerate(refs[: 2 * GROUP]):
            stream, piece = divmod(index, GROUP)
            first_rows = pl.ds(2 * stream * order, order)
            second_rows = pl.ds((2 * stream + 1) * order, order)
            first_lanes = pl.ds(piece * part, part)
            second_lanes = pl.ds(width + piece * part, part)
            for target, real, imag in zip((r_upper, r_lower), split(ref[0]), split(ref[1])):
                target[first_rows, first_lanes] = real
                target[first_rows, second_lanes] = imag
                target[second_rows, first_lanes] = -imag
                target[second_rows, second_lanes] = real

    product = three_pass(upper_ref[...], lower_ref[...], r_upper[...], r_lower[...])
    out_ref[0] = product[:, :width]
    out_ref[1] = product[:, width:]


def block(folded, first, chains, previous=None):
    upper, lower = folded
    row_count, depth = upper.shape
    order = depth // 4
    tile = row_count // 4
    pieces = [chain.piece(first + p) for chain in chains for p in range(GROUP)]
    part = pieces[0].shape[2]
    width = GROUP * part
    left = pl.BlockSpec((tile, depth), lambda i: (i, 0))
    whole = pl.BlockSpec((2, order, part), lambda i: (0, 0, 0))
    operands = [upper, lower] + pieces
    specs = [left, left] + [whole] * len(pieces)
    aliases = {}
    if previous is not None:
        aliases = {len(operands): 0}
        operands.append(previous)
        specs.append(pl.BlockSpec(memory_space=pl.ANY))
    place = first // GROUP
    return pl.pallas_call(
        block_kernel,
        grid=(row_count // tile,),
        in_specs=specs,
        out_specs=pl.BlockSpec((2, tile, width), lambda i: (0, i, place)),
        out_shape=jax.ShapeDtypeStruct((2, row_count, PIECES * part), jnp.float32),
        scratch_shapes=[pltpu.VMEM((depth, 2 * width), jnp.bfloat16)] * 2,
        input_output_aliases=aliases,
        compiler_params=pltpu.CompilerParams(vmem_limit_bytes=VMEM_BYTES),
        cost_estimate=pl.CostEstimate(
            flops=12 * row_count * depth * width,
            bytes_accessed=(4 * depth + 8 * width) * row_count,
            transcendentals=0,
        ),
        name="block",
    )(*operands)


def tie(value, *others):
    return lax.optimization_barrier((value,) + others)[0] if others else value


class Chain:
    def __init__(self, home, row, root, order):
        self.home, self.row, self.order = home, row, order
        self.width = home.shape[2] // PIECES
        place = lax.axis_index("row")
        self.outside = (place == 0) | (place == LINE - 1)
        self.holder = place == root
        beside = ((place == 1) & (root == 0)) | ((place == LINE - 2) & (root == LINE - 1))
        self.way = jnp.where(
            self.holder, 0, jnp.where(self.outside, 3, jnp.where(beside, 1, 2))
        )
        self.outer, self.inner = [], []
        slab = lax.dynamic_slice_in_dim(home, row, order, 1)
        self.own = lax.optimization_barrier(
            [
                lax.slice_in_dim(slab, p * self.width, (p + 1) * self.width, axis=2)
                for p in range(PIECES)
            ]
        )

    def step(self, index, *others):
        ahead = self.own[min(index, PIECES - 1)]
        if index:
            last = self.outer[-1:] + self.inner[-1:]
            ahead, *last = lax.optimization_barrier((ahead, *last, *others))[: 1 + len(last)]
            self.outer[-1] = last[0]
            if self.inner:
                self.inner[-1] = last[1]
        value = ahead
        if index >= 2:
            passing = jnp.where(self.holder, self.own[index - 2], self.inner[index - 2])
            value = jnp.where(self.outside, ahead, passing)
        if 1 <= index <= PIECES:
            crossing = jnp.where(self.holder, self.own[index - 1], self.outer[index - 1])
            self.inner.append(lax.ppermute(crossing, "row", [(1, 2), (2, 1)]))
        self.outer.append(lax.ppermute(value, "row", [(0, 1), (1, 0), (2, 3), (3, 2)]))

    def piece(self, index):
        value = self.outer[index + 2]
        for way, other in ((2, self.inner[index]), (1, self.outer[index]), (0, self.own[index])):
            value = jnp.where(self.way == way, other, value)
        return value


def planned(perambulator, insertion_ops, ins_times, sign_table, perm_table):
    vec_count = insertion_ops.shape[2]
    spins = sign_table.shape[1]
    order = spins * vec_count
    _, row_count, col_count = perambulator.shape
    rows_local = row_count // order
    times_local = col_count // order
    spin_size = lax.axis_size("spin")
    core, side = lax.axis_index("spin"), lax.axis_index("col")
    half_rows = row_count // 2
    exchange = [(0, 1), (1, 0)]

    chains = [
        Chain(
            perambulator,
            ins_times[k] % rows_local * order,
            ins_times[k] // rows_local,
            order,
        )
        for k in range(2)
    ]

    def columns(half):
        return jnp.stack(
            [
                lax.dynamic_slice(
                    perambulator,
                    (0, half * half_rows, ins_times[k] % times_local * order),
                    (2, half_rows, order),
                )
                for k in range(2)
            ]
        )

    owner = ins_times // times_local
    kept = columns(core)
    got = lax.ppermute(columns(1 - core), "spin", exchange)
    mine = jnp.where((owner % spin_size == core)[:, None, None, None], kept, got)
    across = lax.ppermute(mine, "col", exchange)
    settings = jnp.concatenate(
        [
            jnp.stack([core, 0]).astype(jnp.int32),
            sign_table.reshape(-1),
            perm_table.reshape(-1),
        ]
    )
    ops = jnp.tile(insertion_ops, (1, 1, 1, spins))

    result = None
    for index in range(PIECES + 2):
        before = ()
        if index == MINE:
            before = (mine,)
        elif index == COLUMNS:
            came = tie(across, *[chain.outer[-1] for chain in chains])
            chosen = jnp.where((owner // spin_size == side)[:, None, None, None], mine, came)
            before = (chosen,)
        elif index == FOLD:
            other = lax.ppermute(chosen, "spin", exchange)
            before = folded = fold(settings, chosen, other, ops)
        elif index in BLOCKS:
            for first in BLOCKS[index]:
                result = block(folded, first, chains, result)
            before = (result,)
        for chain in chains:
            chain.step(index, *before)
    return block(folded, PIECES - GROUP, chains, result)


def insertion_matrices(insertion_ops, sign_table, perm_table):
    spins = sign_table.shape[1]
    vec_count = insertion_ops.shape[2]
    order = spins * vec_count
    hit = perm_table[:, :, None] == jnp.arange(spins)[None, None, :]
    sign = sign_table[:, :, None]

    def weight(plus, minus):
        value = (sign == plus).astype(jnp.float32) - (sign == minus).astype(jnp.float32)
        return jnp.where(hit, value, 0.0)[:, :, None, :, None]

    real_weight, imag_weight = weight(0, 2), weight(1, 3)
    op_real = insertion_ops[:, 0][:, None, :, None, :]
    op_imag = insertion_ops[:, 1][:, None, :, None, :]
    real = (real_weight * op_real - imag_weight * op_imag).reshape(-1, order, order)
    imag = (real_weight * op_imag + imag_weight * op_real).reshape(-1, order, order)
    return jnp.concatenate(
        [jnp.concatenate([real, imag], axis=2), jnp.concatenate([-imag, real], axis=2)], axis=1
    )


def spread(value, axis, root):
    mine = lax.axis_index(axis) == root
    return lax.psum(jnp.where(mine, value, jnp.zeros_like(value)), axis)


def general(perambulator, insertion_ops, ins_times, sign_table, perm_table):
    vec_count = insertion_ops.shape[2]
    order = sign_table.shape[1] * vec_count
    _, row_count, col_count = perambulator.shape
    piece_rows = min(order, row_count)
    times_local = col_count // order
    gamma = insertion_matrices(insertion_ops, sign_table, perm_table)

    def dot(a, b):
        return jnp.dot(a, b, precision=lax.Precision.HIGHEST)

    real = imag = 0.0
    for k in range(insertion_ops.shape[0]):
        moment = ins_times[k]
        column = spread(
            lax.dynamic_slice_in_dim(perambulator, moment % times_local * order, order, 2),
            ("col", "spin"),
            moment // times_local,
        )
        received = []
        for piece in range(order // piece_rows):
            start = moment * order + piece * piece_rows
            candidate = lax.dynamic_slice_in_dim(perambulator, start % row_count, piece_rows, 1)
            received.append(spread(candidate, "row", start // row_count))
        slab = jnp.concatenate(received, axis=1)
        folded = dot(jnp.concatenate([column[0], column[1]], axis=1), gamma[k])
        left, right = folded[:, :order], folded[:, order:]
        real = real + dot(left, slab[0]) - dot(right, slab[1])
        imag = imag + dot(left, slab[1]) + dot(right, slab[0])
    return jnp.stack([real, imag])


def solution(mesh):
    def shards(perambulator, insertion_ops, ins_times, sign_table, perm_table):
        order = sign_table.shape[1] * insertion_ops.shape[2]
        fits = (
            mesh.shape["row"] == LINE
            and insertion_ops.shape[0] == 2
            and mesh.shape["col"] == 2
            and mesh.shape["spin"] == 2
            and perambulator.shape[1] % order == 0
        )
        arguments = (perambulator, insertion_ops, ins_times, sign_table, perm_table)
        return planned(*arguments) if fits else general(*arguments)

    return jax.shard_map(
        shards,
        mesh=mesh,
        in_specs=(P(None, ("cfg", "row"), ("col", "spin")), P(), P(), P(), P()),
        out_specs=P(None, ("cfg", "row"), ("col", "spin")),
        check_vma=False,
    )
```

```python
import functools

import jax
import jax.numpy as jnp
from jax import lax
from jax.experimental import pallas as pl
from jax.experimental.pallas import tpu as pltpu
from jax.sharding import PartitionSpec as P

VMEM_BYTES = 40 * 1024 * 1024
LINE = 4
PIECES = 8
GROUP = 2
MINE, COLUMNS, FOLD = 1, 5, 7
BLOCKS = {8: (0,), 9: (2, 4)}


def split(value):
    upper = value.astype(jnp.bfloat16)
    lower = (value - upper.astype(jnp.float32)).astype(jnp.bfloat16)
    return upper, lower


def three_pass(a_upper, a_lower, b_upper, b_lower):
    def dot(a, b):
        return jnp.dot(a, b, preferred_element_type=jnp.float32)

    return dot(a_upper, b_upper) + (dot(a_upper, b_lower) + dot(a_lower, b_upper))


def fold_kernel(numbers, own_ref, other_ref, op_ref, upper_ref, lower_ref, g_upper, g_lower):
    stream, half = pl.program_id(0), pl.program_id(1)
    vec_count, order = op_ref.shape[2:]
    spins = order // vec_count
    insertion = jnp.where(numbers[1] == 1, 1 - stream, stream)

    @pl.when((half == 0) & (pl.program_id(2) == 0))
    def _():
        lane_spin = lax.broadcasted_iota(jnp.int32, (vec_count, order), 1) // vec_count
        op_real, op_imag = op_ref[insertion, 0], op_ref[insertion, 1]
        for spin in range(spins):
            sign = numbers[2 + insertion * spins + spin]
            column = numbers[2 + (2 + insertion) * spins + spin]
            hit = lane_spin == column
            odd = (sign == 1) | (sign == 3)
            flip = jnp.where(sign >= 2, -1.0, 1.0)
            real = jnp.where(hit, flip * jnp.where(odd, -op_imag, op_real), 0.0)
            imag = jnp.where(hit, flip * jnp.where(odd, op_real, op_imag), 0.0)
            real_parts, imag_parts = split(real), split(imag)
            first = pl.ds(spin * vec_count, vec_count)
            second = pl.ds(order + spin * vec_count, vec_count)
            for ref, part_real, part_imag in zip((g_upper, g_lower), real_parts, imag_parts):
                ref[first, :order] = part_real
                ref[first, order:] = part_imag
                ref[second, :order] = -part_imag
                ref[second, order:] = part_real

    mine = numbers[0] == half
    joined = jnp.concatenate(
        [
            jnp.where(mine, own_ref[0, 0], other_ref[0, 0]),
            jnp.where(mine, own_ref[0, 1], other_ref[0, 1]),
        ],
        axis=1,
    )
    product = three_pass(*split(joined), g_upper[...], g_lower[...])
    upper_ref[...], lower_ref[...] = split(product)


def fold(numbers, own, other, ops):
    streams, _, rows, order = own.shape
    tile = rows
    shape = jax.ShapeDtypeStruct((2 * rows, streams * 2 * order), jnp.bfloat16)
    slab_spec = pl.BlockSpec((1, 2, tile, order), lambda k, h, i, numbers: (k, 0, i, 0))
    out_spec = pl.BlockSpec((tile, 2 * order), lambda k, h, i, numbers: (h + i, k))
    return pl.pallas_call(
        fold_kernel,
        grid_spec=pltpu.PrefetchScalarGridSpec(
            num_scalar_prefetch=1,
            grid=(streams, 2, 1),
            in_specs=[
                slab_spec,
                slab_spec,
                pl.BlockSpec(ops.shape, lambda k, h, i, numbers: (0, 0, 0, 0)),
            ],
            out_specs=[out_spec, out_spec],
            scratch_shapes=[pltpu.VMEM((2 * order, 2 * order), jnp.bfloat16)] * 2,
        ),
        out_shape=[shape, shape],
        compiler_params=pltpu.CompilerParams(vmem_limit_bytes=VMEM_BYTES),
        cost_estimate=pl.CostEstimate(
            flops=24 * streams * 2 * rows * order * 2 * order,
            bytes_accessed=16 * own.size,
            transcendentals=0,
        ),
        name="fold",
    )(numbers, own, other, ops)


def block_kernel(upper_ref, lower_ref, *refs):
    out_ref, r_upper, r_lower = refs[-3:]
    order = refs[0].shape[1]
    part = refs[0].shape[2]
    width = GROUP * part

    @pl.when(pl.program_id(0) == 0)
    def _():
        for index, ref in enumerate(refs[: 2 * GROUP]):
            stream, piece = divmod(index, GROUP)
            first_rows = pl.ds(2 * stream * order, order)
            second_rows = pl.ds((2 * stream + 1) * order, order)
            first_lanes = pl.ds(piece * part, part)
            second_lanes = pl.ds(width + piece * part, part)
            for target, real, imag in zip((r_upper, r_lower), split(ref[0]), split(ref[1])):
                target[first_rows, first_lanes] = real
                target[first_rows, second_lanes] = imag
                target[second_rows, first_lanes] = -imag
                target[second_rows, second_lanes] = real

    product = three_pass(upper_ref[...], lower_ref[...], r_upper[...], r_lower[...])
    out_ref[0] = product[:, :width]
    out_ref[1] = product[:, width:]


def block(folded, first, chains, previous=None):
    upper, lower = folded
    row_count, depth = upper.shape
    order = depth // 4
    tile = row_count // 4
    pieces = [chain.piece(first + p) for chain in chains for p in range(GROUP)]
    part = pieces[0].shape[2]
    width = GROUP * part
    left = pl.BlockSpec((tile, depth), lambda i: (i, 0))
    whole = pl.BlockSpec((2, order, part), lambda i: (0, 0, 0))
    operands = [upper, lower] + pieces
    specs = [left, left] + [whole] * len(pieces)
    aliases = {}
    if previous is not None:
        aliases = {len(operands): 0}
        operands.append(previous)
        specs.append(pl.BlockSpec(memory_space=pl.ANY))
    place = first // GROUP
    return pl.pallas_call(
        block_kernel,
        grid=(row_count // tile,),
        in_specs=specs,
        out_specs=pl.BlockSpec((2, tile, width), lambda i: (0, i, place)),
        out_shape=jax.ShapeDtypeStruct((2, row_count, PIECES * part), jnp.float32),
        scratch_shapes=[pltpu.VMEM((depth, 2 * width), jnp.bfloat16)] * 2,
        input_output_aliases=aliases,
        compiler_params=pltpu.CompilerParams(vmem_limit_bytes=VMEM_BYTES),
        cost_estimate=pl.CostEstimate(
            flops=12 * row_count * depth * width,
            bytes_accessed=(4 * depth + 8 * width) * row_count,
            transcendentals=0,
        ),
        name="block",
    )(*operands)


def tie(value, *others):
    return lax.optimization_barrier((value,) + others)[0] if others else value


class Chain:
    def __init__(self, home, row, root, order):
        self.home, self.row, self.order = home, row, order
        self.width = home.shape[2] // PIECES
        place = lax.axis_index("row")
        self.outside = (place == 0) | (place == LINE - 1)
        self.holder = place == root
        beside = ((place == 1) & (root == 0)) | ((place == LINE - 2) & (root == LINE - 1))
        self.way = jnp.where(
            self.holder, 0, jnp.where(self.outside, 3, jnp.where(beside, 1, 2))
        )
        self.outer, self.inner = [], []
        slab = lax.dynamic_slice_in_dim(home, row, order, 1)
        self.own = lax.optimization_barrier(
            [
                lax.slice_in_dim(slab, p * self.width, (p + 1) * self.width, axis=2)
                for p in range(PIECES)
            ]
        )

    def step(self, index, *others):
        ahead = self.own[min(index, PIECES - 1)]
        if index:
            last = self.outer[-1:] + self.inner[-1:]
            ahead, *last = lax.optimization_barrier((ahead, *last, *others))[: 1 + len(last)]
            self.outer[-1] = last[0]
            if self.inner:
                self.inner[-1] = last[1]
        value = ahead
        if index >= 2:
            passing = jnp.where(self.holder, self.own[index - 2], self.inner[index - 2])
            value = jnp.where(self.outside, ahead, passing)
        if 1 <= index <= PIECES:
            crossing = jnp.where(self.holder, self.own[index - 1], self.outer[index - 1])
            self.inner.append(lax.ppermute(crossing, "row", [(1, 2), (2, 1)]))
        self.outer.append(lax.ppermute(value, "row", [(0, 1), (1, 0), (2, 3), (3, 2)]))

    def piece(self, index):
        value = self.outer[index + 2]
        for way, other in ((2, self.inner[index]), (1, self.outer[index]), (0, self.own[index])):
            value = jnp.where(self.way == way, other, value)
        return value


def planned(perambulator, insertion_ops, ins_times, sign_table, perm_table):
    vec_count = insertion_ops.shape[2]
    spins = sign_table.shape[1]
    order = spins * vec_count
    _, row_count, col_count = perambulator.shape
    rows_local = row_count // order
    times_local = col_count // order
    spin_size = lax.axis_size("spin")
    core, side = lax.axis_index("spin"), lax.axis_index("col")
    half_rows = row_count // 2
    exchange = [(0, 1), (1, 0)]

    chains = [
        Chain(
            perambulator,
            ins_times[k] % rows_local * order,
            ins_times[k] // rows_local,
            order,
        )
        for k in range(2)
    ]

    def columns(half):
        return jnp.stack(
            [
                lax.dynamic_slice(
                    perambulator,
                    (0, half * half_rows, ins_times[k] % times_local * order),
                    (2, half_rows, order),
                )
                for k in range(2)
            ]
        )

    owner = ins_times // times_local
    kept = columns(core)
    got = lax.ppermute(columns(1 - core), "spin", exchange)
    mine = jnp.where((owner % spin_size == core)[:, None, None, None], kept, got)
    across = lax.ppermute(mine, "col", exchange)
    settings = jnp.concatenate(
        [
            jnp.stack([core, 0]).astype(jnp.int32),
            sign_table.reshape(-1),
            perm_table.reshape(-1),
        ]
    )
    ops = jnp.tile(insertion_ops, (1, 1, 1, spins))

    result = None
    for index in range(PIECES + 2):
        before = ()
        if index == MINE:
            before = (mine,)
        elif index == COLUMNS:
            came = tie(across, *[chain.outer[-1] for chain in chains])
            chosen = jnp.where((owner // spin_size == side)[:, None, None, None], mine, came)
            before = (chosen,)
        elif index == FOLD:
            other = lax.ppermute(chosen, "spin", exchange)
            before = folded = fold(settings, chosen, other, ops)
        elif index in BLOCKS:
            for first in BLOCKS[index]:
                result = block(folded, first, chains, result)
            before = (result,)
        for chain in chains:
            chain.step(index, *before)
    return block(folded, PIECES - GROUP, chains, result)


def insertion_matrices(insertion_ops, sign_table, perm_table):
    spins = sign_table.shape[1]
    vec_count = insertion_ops.shape[2]
    order = spins * vec_count
    hit = perm_table[:, :, None] == jnp.arange(spins)[None, None, :]
    sign = sign_table[:, :, None]

    def weight(plus, minus):
        value = (sign == plus).astype(jnp.float32) - (sign == minus).astype(jnp.float32)
        return jnp.where(hit, value, 0.0)[:, :, None, :, None]

    real_weight, imag_weight = weight(0, 2), weight(1, 3)
    op_real = insertion_ops[:, 0][:, None, :, None, :]
    op_imag = insertion_ops[:, 1][:, None, :, None, :]
    real = (real_weight * op_real - imag_weight * op_imag).reshape(-1, order, order)
    imag = (real_weight * op_imag + imag_weight * op_real).reshape(-1, order, order)
    return jnp.concatenate(
        [jnp.concatenate([real, imag], axis=2), jnp.concatenate([-imag, real], axis=2)], axis=1
    )


def spread(value, axis, root):
    mine = lax.axis_index(axis) == root
    return lax.psum(jnp.where(mine, value, jnp.zeros_like(value)), axis)


def general(perambulator, insertion_ops, ins_times, sign_table, perm_table):
    vec_count = insertion_ops.shape[2]
    order = sign_table.shape[1] * vec_count
    _, row_count, col_count = perambulator.shape
    piece_rows = min(order, row_count)
    times_local = col_count // order
    gamma = insertion_matrices(insertion_ops, sign_table, perm_table)

    def dot(a, b):
        return jnp.dot(a, b, precision=lax.Precision.HIGHEST)

    real = imag = 0.0
    for k in range(insertion_ops.shape[0]):
        moment = ins_times[k]
        column = spread(
            lax.dynamic_slice_in_dim(perambulator, moment % times_local * order, order, 2),
            ("col", "spin"),
            moment // times_local,
        )
        received = []
        for piece in range(order // piece_rows):
            start = moment * order + piece * piece_rows
            candidate = lax.dynamic_slice_in_dim(perambulator, start % row_count, piece_rows, 1)
            received.append(spread(candidate, "row", start // row_count))
        slab = jnp.concatenate(received, axis=1)
        folded = dot(jnp.concatenate([column[0], column[1]], axis=1), gamma[k])
        left, right = folded[:, :order], folded[:, order:]
        real = real + dot(left, slab[0]) - dot(right, slab[1])
        imag = imag + dot(left, slab[1]) + dot(right, slab[0])
    return jnp.stack([real, imag])


def solution(mesh):
    def shards(perambulator, insertion_ops, ins_times, sign_table, perm_table):
        order = sign_table.shape[1] * insertion_ops.shape[2]
        fits = (
            mesh.shape["row"] == LINE
            and insertion_ops.shape[0] == 2
            and mesh.shape["col"] == 2
            and mesh.shape["spin"] == 2
            and perambulator.shape[1] % order == 0
        )
        arguments = (perambulator, insertion_ops, ins_times, sign_table, perm_table)
        return planned(*arguments) if fits else general(*arguments)

    return jax.shard_map(
        shards,
        mesh=mesh,
        in_specs=(P(None, ("cfg", "row"), ("col", "spin")), P(), P(), P(), P()),
        out_specs=P(None, ("cfg", "row"), ("col", "spin")),
        check_vma=False,
    )
```

```python
import functools

import jax
import jax.numpy as jnp
from jax import lax
from jax.experimental import pallas as pl
from jax.experimental.pallas import tpu as pltpu
from jax.sharding import PartitionSpec as P

VMEM_BYTES = 40 * 1024 * 1024
LINE = 4
PIECES = 8
GROUP = 2
MINE, COLUMNS, FOLD = 1, 5, 7
BLOCKS = {9: (0, 2)}


def split(value):
    upper = value.astype(jnp.bfloat16)
    lower = (value - upper.astype(jnp.float32)).astype(jnp.bfloat16)
    return upper, lower


def three_pass(a_upper, a_lower, b_upper, b_lower):
    def dot(a, b):
        return jnp.dot(a, b, preferred_element_type=jnp.float32)

    return dot(a_upper, b_upper) + (dot(a_upper, b_lower) + dot(a_lower, b_upper))


def fold_kernel(numbers, own_ref, other_ref, op_ref, upper_ref, lower_ref, g_upper, g_lower):
    stream, half = pl.program_id(0), pl.program_id(1)
    vec_count, order = op_ref.shape[2:]
    spins = order // vec_count
    insertion = jnp.where(numbers[1] == 1, 1 - stream, stream)

    @pl.when((half == 0) & (pl.program_id(2) == 0))
    def _():
        lane_spin = lax.broadcasted_iota(jnp.int32, (vec_count, order), 1) // vec_count
        op_real, op_imag = op_ref[insertion, 0], op_ref[insertion, 1]
        for spin in range(spins):
            sign = numbers[2 + insertion * spins + spin]
            column = numbers[2 + (2 + insertion) * spins + spin]
            hit = lane_spin == column
            odd = (sign == 1) | (sign == 3)
            flip = jnp.where(sign >= 2, -1.0, 1.0)
            real = jnp.where(hit, flip * jnp.where(odd, -op_imag, op_real), 0.0)
            imag = jnp.where(hit, flip * jnp.where(odd, op_real, op_imag), 0.0)
            real_parts, imag_parts = split(real), split(imag)
            first = pl.ds(spin * vec_count, vec_count)
            second = pl.ds(order + spin * vec_count, vec_count)
            for ref, part_real, part_imag in zip((g_upper, g_lower), real_parts, imag_parts):
                ref[first, :order] = part_real
                ref[first, order:] = part_imag
                ref[second, :order] = -part_imag
                ref[second, order:] = part_real

    mine = numbers[0] == half
    joined = jnp.concatenate(
        [
            jnp.where(mine, own_ref[0, 0], other_ref[0, 0]),
            jnp.where(mine, own_ref[0, 1], other_ref[0, 1]),
        ],
        axis=1,
    )
    product = three_pass(*split(joined), g_upper[...], g_lower[...])
    upper_ref[...], lower_ref[...] = split(product)


def fold(numbers, own, other, ops):
    streams, _, rows, order = own.shape
    tile = rows
    shape = jax.ShapeDtypeStruct((2 * rows, streams * 2 * order), jnp.bfloat16)
    slab_spec = pl.BlockSpec((1, 2, tile, order), lambda k, h, i, numbers: (k, 0, i, 0))
    out_spec = pl.BlockSpec((tile, 2 * order), lambda k, h, i, numbers: (h + i, k))
    return pl.pallas_call(
        fold_kernel,
        grid_spec=pltpu.PrefetchScalarGridSpec(
            num_scalar_prefetch=1,
            grid=(streams, 2, 1),
            in_specs=[
                slab_spec,
                slab_spec,
                pl.BlockSpec(ops.shape, lambda k, h, i, numbers: (0, 0, 0, 0)),
            ],
            out_specs=[out_spec, out_spec],
            scratch_shapes=[pltpu.VMEM((2 * order, 2 * order), jnp.bfloat16)] * 2,
        ),
        out_shape=[shape, shape],
        compiler_params=pltpu.CompilerParams(vmem_limit_bytes=VMEM_BYTES),
        cost_estimate=pl.CostEstimate(
            flops=24 * streams * 2 * rows * order * 2 * order,
            bytes_accessed=16 * own.size,
            transcendentals=0,
        ),
        name="fold",
    )(numbers, own, other, ops)


def block_kernel(upper_ref, lower_ref, *refs):
    out_ref, r_upper, r_lower = refs[-3:]
    order = refs[0].shape[1]
    part = refs[0].shape[2]
    width = GROUP * part

    @pl.when(pl.program_id(0) == 0)
    def _():
        for index, ref in enumerate(refs[: 2 * GROUP]):
            stream, piece = divmod(index, GROUP)
            first_rows = pl.ds(2 * stream * order, order)
            second_rows = pl.ds((2 * stream + 1) * order, order)
            first_lanes = pl.ds(piece * part, part)
            second_lanes = pl.ds(width + piece * part, part)
            for target, real, imag in zip((r_upper, r_lower), split(ref[0]), split(ref[1])):
                target[first_rows, first_lanes] = real
                target[first_rows, second_lanes] = imag
                target[second_rows, first_lanes] = -imag
                target[second_rows, second_lanes] = real

    product = three_pass(upper_ref[...], lower_ref[...], r_upper[...], r_lower[...])
    out_ref[0] = product[:, :width]
    out_ref[1] = product[:, width:]


def block(folded, first, chains, previous=None):
    upper, lower = folded
    row_count, depth = upper.shape
    order = depth // 4
    tile = row_count // 4
    pieces = [chain.piece(first + p) for chain in chains for p in range(GROUP)]
    part = pieces[0].shape[2]
    width = GROUP * part
    left = pl.BlockSpec((tile, depth), lambda i: (i, 0))
    whole = pl.BlockSpec((2, order, part), lambda i: (0, 0, 0))
    operands = [upper, lower] + pieces
    specs = [left, left] + [whole] * len(pieces)
    aliases = {}
    if previous is not None:
        aliases = {len(operands): 0}
        operands.append(previous)
        specs.append(pl.BlockSpec(memory_space=pl.ANY))
    place = first // GROUP
    return pl.pallas_call(
        block_kernel,
        grid=(row_count // tile,),
        in_specs=specs,
        out_specs=pl.BlockSpec((2, tile, width), lambda i: (0, i, place)),
        out_shape=jax.ShapeDtypeStruct((2, row_count, PIECES * part), jnp.float32),
        scratch_shapes=[pltpu.VMEM((depth, 2 * width), jnp.bfloat16)] * 2,
        input_output_aliases=aliases,
        compiler_params=pltpu.CompilerParams(vmem_limit_bytes=VMEM_BYTES),
        cost_estimate=pl.CostEstimate(
            flops=12 * row_count * depth * width,
            bytes_accessed=(4 * depth + 8 * width) * row_count,
            transcendentals=0,
        ),
        name="block",
    )(*operands)


def tie(value, *others):
    return lax.optimization_barrier((value,) + others)[0] if others else value


class Chain:
    def __init__(self, home, row, root, order):
        self.home, self.row, self.order = home, row, order
        self.width = home.shape[2] // PIECES
        place = lax.axis_index("row")
        self.outside = (place == 0) | (place == LINE - 1)
        self.holder = place == root
        beside = ((place == 1) & (root == 0)) | ((place == LINE - 2) & (root == LINE - 1))
        self.way = jnp.where(
            self.holder, 0, jnp.where(self.outside, 3, jnp.where(beside, 1, 2))
        )
        self.outer, self.inner = [], []
        slab = lax.dynamic_slice_in_dim(home, row, order, 1)
        self.own = lax.optimization_barrier(
            [
                lax.slice_in_dim(slab, p * self.width, (p + 1) * self.width, axis=2)
                for p in range(PIECES)
            ]
        )

    def step(self, index, *others):
        ahead = self.own[min(index, PIECES - 1)]
        if index:
            last = self.outer[-1:] + self.inner[-1:]
            ahead, *last = lax.optimization_barrier((ahead, *last, *others))[: 1 + len(last)]
            self.outer[-1] = last[0]
            if self.inner:
                self.inner[-1] = last[1]
        value = ahead
        if index >= 2:
            passing = jnp.where(self.holder, self.own[index - 2], self.inner[index - 2])
            value = jnp.where(self.outside, ahead, passing)
        if 1 <= index <= PIECES:
            crossing = jnp.where(self.holder, self.own[index - 1], self.outer[index - 1])
            self.inner.append(lax.ppermute(crossing, "row", [(1, 2), (2, 1)]))
        self.outer.append(lax.ppermute(value, "row", [(0, 1), (1, 0), (2, 3), (3, 2)]))

    def piece(self, index):
        value = self.outer[index + 2]
        for way, other in ((2, self.inner[index]), (1, self.outer[index]), (0, self.own[index])):
            value = jnp.where(self.way == way, other, value)
        return value


def planned(perambulator, insertion_ops, ins_times, sign_table, perm_table):
    vec_count = insertion_ops.shape[2]
    spins = sign_table.shape[1]
    order = spins * vec_count
    _, row_count, col_count = perambulator.shape
    rows_local = row_count // order
    times_local = col_count // order
    spin_size = lax.axis_size("spin")
    core, side = lax.axis_index("spin"), lax.axis_index("col")
    half_rows = row_count // 2
    exchange = [(0, 1), (1, 0)]

    chains = [
        Chain(
            perambulator,
            ins_times[k] % rows_local * order,
            ins_times[k] // rows_local,
            order,
        )
        for k in range(2)
    ]

    def columns(half):
        return jnp.stack(
            [
                lax.dynamic_slice(
                    perambulator,
                    (0, half * half_rows, ins_times[k] % times_local * order),
                    (2, half_rows, order),
                )
                for k in range(2)
            ]
        )

    owner = ins_times // times_local
    kept = columns(core)
    got = lax.ppermute(columns(1 - core), "spin", exchange)
    mine = jnp.where((owner % spin_size == core)[:, None, None, None], kept, got)
    across = lax.ppermute(mine, "col", exchange)
    settings = jnp.concatenate(
        [
            jnp.stack([core, 0]).astype(jnp.int32),
            sign_table.reshape(-1),
            perm_table.reshape(-1),
        ]
    )
    ops = jnp.tile(insertion_ops, (1, 1, 1, spins))

    result = None
    for index in range(PIECES + 2):
        before = ()
        if index == MINE:
            before = (mine,)
        elif index == COLUMNS:
            came = tie(across, *[chain.outer[-1] for chain in chains])
            chosen = jnp.where((owner // spin_size == side)[:, None, None, None], mine, came)
            before = (chosen,)
        elif index == FOLD:
            other = lax.ppermute(chosen, "spin", exchange)
            before = folded = fold(settings, chosen, other, ops)
        elif index in BLOCKS:
            for first in BLOCKS[index]:
                result = block(folded, first, chains, result)
            before = (result,)
        for chain in chains:
            chain.step(index, *before)
    result = block(folded, PIECES - 2 * GROUP, chains, result)
    return block(folded, PIECES - GROUP, chains, result)


def insertion_matrices(insertion_ops, sign_table, perm_table):
    spins = sign_table.shape[1]
    vec_count = insertion_ops.shape[2]
    order = spins * vec_count
    hit = perm_table[:, :, None] == jnp.arange(spins)[None, None, :]
    sign = sign_table[:, :, None]

    def weight(plus, minus):
        value = (sign == plus).astype(jnp.float32) - (sign == minus).astype(jnp.float32)
        return jnp.where(hit, value, 0.0)[:, :, None, :, None]

    real_weight, imag_weight = weight(0, 2), weight(1, 3)
    op_real = insertion_ops[:, 0][:, None, :, None, :]
    op_imag = insertion_ops[:, 1][:, None, :, None, :]
    real = (real_weight * op_real - imag_weight * op_imag).reshape(-1, order, order)
    imag = (real_weight * op_imag + imag_weight * op_real).reshape(-1, order, order)
    return jnp.concatenate(
        [jnp.concatenate([real, imag], axis=2), jnp.concatenate([-imag, real], axis=2)], axis=1
    )


def spread(value, axis, root):
    mine = lax.axis_index(axis) == root
    return lax.psum(jnp.where(mine, value, jnp.zeros_like(value)), axis)


def general(perambulator, insertion_ops, ins_times, sign_table, perm_table):
    vec_count = insertion_ops.shape[2]
    order = sign_table.shape[1] * vec_count
    _, row_count, col_count = perambulator.shape
    piece_rows = min(order, row_count)
    times_local = col_count // order
    gamma = insertion_matrices(insertion_ops, sign_table, perm_table)

    def dot(a, b):
        return jnp.dot(a, b, precision=lax.Precision.HIGHEST)

    real = imag = 0.0
    for k in range(insertion_ops.shape[0]):
        moment = ins_times[k]
        column = spread(
            lax.dynamic_slice_in_dim(perambulator, moment % times_local * order, order, 2),
            ("col", "spin"),
            moment // times_local,
        )
        received = []
        for piece in range(order // piece_rows):
            start = moment * order + piece * piece_rows
            candidate = lax.dynamic_slice_in_dim(perambulator, start % row_count, piece_rows, 1)
            received.append(spread(candidate, "row", start // row_count))
        slab = jnp.concatenate(received, axis=1)
        folded = dot(jnp.concatenate([column[0], column[1]], axis=1), gamma[k])
        left, right = folded[:, :order], folded[:, order:]
        real = real + dot(left, slab[0]) - dot(right, slab[1])
        imag = imag + dot(left, slab[1]) + dot(right, slab[0])
    return jnp.stack([real, imag])


def solution(mesh):
    def shards(perambulator, insertion_ops, ins_times, sign_table, perm_table):
        order = sign_table.shape[1] * insertion_ops.shape[2]
        fits = (
            mesh.shape["row"] == LINE
            and insertion_ops.shape[0] == 2
            and mesh.shape["col"] == 2
            and mesh.shape["spin"] == 2
            and perambulator.shape[1] % order == 0
        )
        arguments = (perambulator, insertion_ops, ins_times, sign_table, perm_table)
        return planned(*arguments) if fits else general(*arguments)

    return jax.shard_map(
        shards,
        mesh=mesh,
        in_specs=(P(None, ("cfg", "row"), ("col", "spin")), P(), P(), P(), P()),
        out_specs=P(None, ("cfg", "row"), ("col", "spin")),
        check_vma=False,
    )
```

```python
import functools

import jax
import jax.numpy as jnp
from jax import lax
from jax.experimental import pallas as pl
from jax.experimental.pallas import tpu as pltpu
from jax.sharding import PartitionSpec as P

VMEM_BYTES = 40 * 1024 * 1024
LINE = 4
PIECES = 8
GROUP = 2
MINE, COLUMNS, FOLD = 1, 5, 7
BLOCKS = {9: (0, 2)}


def split(value):
    upper = value.astype(jnp.bfloat16)
    lower = (value - upper.astype(jnp.float32)).astype(jnp.bfloat16)
    return upper, lower


def three_pass(a_upper, a_lower, b_upper, b_lower):
    def dot(a, b):
        return jnp.dot(a, b, preferred_element_type=jnp.float32)

    return dot(a_upper, b_upper) + (dot(a_upper, b_lower) + dot(a_lower, b_upper))


def fold_kernel(numbers, own_ref, other_ref, op_ref, upper_ref, lower_ref, g_upper, g_lower):
    stream, half = pl.program_id(0), pl.program_id(1)
    vec_count, order = op_ref.shape[2:]
    spins = order // vec_count
    insertion = jnp.where(numbers[1] == 1, 1 - stream, stream)

    @pl.when((half == 0) & (pl.program_id(2) == 0))
    def _():
        lane_spin = lax.broadcasted_iota(jnp.int32, (vec_count, order), 1) // vec_count
        op_real, op_imag = op_ref[insertion, 0], op_ref[insertion, 1]
        for spin in range(spins):
            sign = numbers[2 + insertion * spins + spin]
            column = numbers[2 + (2 + insertion) * spins + spin]
            hit = lane_spin == column
            odd = (sign == 1) | (sign == 3)
            flip = jnp.where(sign >= 2, -1.0, 1.0)
            real = jnp.where(hit, flip * jnp.where(odd, -op_imag, op_real), 0.0)
            imag = jnp.where(hit, flip * jnp.where(odd, op_real, op_imag), 0.0)
            real_parts, imag_parts = split(real), split(imag)
            first = pl.ds(spin * vec_count, vec_count)
            second = pl.ds(order + spin * vec_count, vec_count)
            for ref, part_real, part_imag in zip((g_upper, g_lower), real_parts, imag_parts):
                ref[first, :order] = part_real
                ref[first, order:] = part_imag
                ref[second, :order] = -part_imag
                ref[second, order:] = part_real

    mine = numbers[0] == half
    joined = jnp.concatenate(
        [
            jnp.where(mine, own_ref[0, 0], other_ref[0, 0]),
            jnp.where(mine, own_ref[0, 1], other_ref[0, 1]),
        ],
        axis=1,
    )
    product = three_pass(*split(joined), g_upper[...], g_lower[...])
    upper_ref[...], lower_ref[...] = split(product)


def fold(numbers, own, other, ops):
    streams, _, rows, order = own.shape
    tile = rows
    shape = jax.ShapeDtypeStruct((2 * rows, streams * 2 * order), jnp.bfloat16)
    slab_spec = pl.BlockSpec((1, 2, tile, order), lambda k, h, i, numbers: (k, 0, i, 0))
    out_spec = pl.BlockSpec((tile, 2 * order), lambda k, h, i, numbers: (h + i, k))
    return pl.pallas_call(
        fold_kernel,
        grid_spec=pltpu.PrefetchScalarGridSpec(
            num_scalar_prefetch=1,
            grid=(streams, 2, 1),
            in_specs=[
                slab_spec,
                slab_spec,
                pl.BlockSpec(ops.shape, lambda k, h, i, numbers: (0, 0, 0, 0)),
            ],
            out_specs=[out_spec, out_spec],
            scratch_shapes=[pltpu.VMEM((2 * order, 2 * order), jnp.bfloat16)] * 2,
        ),
        out_shape=[shape, shape],
        compiler_params=pltpu.CompilerParams(vmem_limit_bytes=VMEM_BYTES),
        cost_estimate=pl.CostEstimate(
            flops=24 * streams * 2 * rows * order * 2 * order,
            bytes_accessed=16 * own.size,
            transcendentals=0,
        ),
        name="fold",
    )(numbers, own, other, ops)


def block_kernel(upper_ref, lower_ref, *refs):
    out_ref, r_upper, r_lower = refs[-3:]
    order = refs[0].shape[1]
    part = refs[0].shape[2]
    width = GROUP * part

    @pl.when(pl.program_id(0) == 0)
    def _():
        for index, ref in enumerate(refs[: 2 * GROUP]):
            stream, piece = divmod(index, GROUP)
            first_rows = pl.ds(2 * stream * order, order)
            second_rows = pl.ds((2 * stream + 1) * order, order)
            first_lanes = pl.ds(piece * part, part)
            second_lanes = pl.ds(width + piece * part, part)
            for target, real, imag in zip((r_upper, r_lower), split(ref[0]), split(ref[1])):
                target[first_rows, first_lanes] = real
                target[first_rows, second_lanes] = imag
                target[second_rows, first_lanes] = -imag
                target[second_rows, second_lanes] = real

    product = three_pass(upper_ref[...], lower_ref[...], r_upper[...], r_lower[...])
    out_ref[0] = product[:, :width]
    out_ref[1] = product[:, width:]


def block(folded, first, chains, previous=None):
    upper, lower = folded
    row_count, depth = upper.shape
    order = depth // 4
    tile = row_count // 4
    pieces = [chain.piece(first + p) for chain in chains for p in range(GROUP)]
    part = pieces[0].shape[2]
    width = GROUP * part
    left = pl.BlockSpec((tile, depth), lambda i: (i, 0))
    whole = pl.BlockSpec((2, order, part), lambda i: (0, 0, 0))
    operands = [upper, lower] + pieces
    specs = [left, left] + [whole] * len(pieces)
    aliases = {}
    if previous is not None:
        aliases = {len(operands): 0}
        operands.append(previous)
        specs.append(pl.BlockSpec(memory_space=pl.ANY))
    place = first // GROUP
    return pl.pallas_call(
        block_kernel,
        grid=(row_count // tile,),
        in_specs=specs,
        out_specs=pl.BlockSpec((2, tile, width), lambda i: (0, i, place)),
        out_shape=jax.ShapeDtypeStruct((2, row_count, PIECES * part), jnp.float32),
        scratch_shapes=[pltpu.VMEM((depth, 2 * width), jnp.bfloat16)] * 2,
        input_output_aliases=aliases,
        compiler_params=pltpu.CompilerParams(vmem_limit_bytes=VMEM_BYTES),
        cost_estimate=pl.CostEstimate(
            flops=12 * row_count * depth * width,
            bytes_accessed=(4 * depth + 8 * width) * row_count,
            transcendentals=0,
        ),
        name="block",
    )(*operands)


def tie(value, *others):
    return lax.optimization_barrier((value,) + others)[0] if others else value


class Chain:
    def __init__(self, home, row, root, order):
        self.home, self.row, self.order = home, row, order
        self.width = home.shape[2] // PIECES
        place = lax.axis_index("row")
        self.outside = (place == 0) | (place == LINE - 1)
        self.holder = place == root
        beside = ((place == 1) & (root == 0)) | ((place == LINE - 2) & (root == LINE - 1))
        self.way = jnp.where(
            self.holder, 0, jnp.where(self.outside, 3, jnp.where(beside, 1, 2))
        )
        self.outer, self.inner = [], []
        slab = lax.dynamic_slice_in_dim(home, row, order, 1)
        self.own = lax.optimization_barrier(
            [
                lax.slice_in_dim(slab, p * self.width, (p + 1) * self.width, axis=2)
                for p in range(PIECES)
            ]
        )

    def step(self, index, *others):
        ahead = self.own[min(index, PIECES - 1)]
        if index:
            last = self.outer[-1:] + self.inner[-1:]
            ahead, *last = lax.optimization_barrier((ahead, *last, *others))[: 1 + len(last)]
            self.outer[-1] = last[0]
            if self.inner:
                self.inner[-1] = last[1]
        value = ahead
        if index >= 2:
            passing = jnp.where(self.holder, self.own[index - 2], self.inner[index - 2])
            value = jnp.where(self.outside, ahead, passing)
        if 1 <= index <= PIECES:
            crossing = jnp.where(self.holder, self.own[index - 1], self.outer[index - 1])
            self.inner.append(lax.ppermute(crossing, "row", [(1, 2), (2, 1)]))
        self.outer.append(lax.ppermute(value, "row", [(0, 1), (1, 0), (2, 3), (3, 2)]))

    def piece(self, index):
        value = self.outer[index + 2]
        for way, other in ((2, self.inner[index]), (1, self.outer[index]), (0, self.own[index])):
            value = jnp.where(self.way == way, other, value)
        return value


def planned(perambulator, insertion_ops, ins_times, sign_table, perm_table):
    vec_count = insertion_ops.shape[2]
    spins = sign_table.shape[1]
    order = spins * vec_count
    _, row_count, col_count = perambulator.shape
    rows_local = row_count // order
    times_local = col_count // order
    spin_size = lax.axis_size("spin")
    core, side = lax.axis_index("spin"), lax.axis_index("col")
    half_rows = row_count // 2
    exchange = [(0, 1), (1, 0)]

    chains = [
        Chain(
            perambulator,
            ins_times[k] % rows_local * order,
            ins_times[k] // rows_local,
            order,
        )
        for k in range(2)
    ]

    def columns(half):
        return jnp.stack(
            [
                lax.dynamic_slice(
                    perambulator,
                    (0, half * half_rows, ins_times[k] % times_local * order),
                    (2, half_rows, order),
                )
                for k in range(2)
            ]
        )

    owner = ins_times // times_local
    kept = columns(core)
    got = lax.ppermute(columns(1 - core), "spin", exchange)
    mine = jnp.where((owner % spin_size == core)[:, None, None, None], kept, got)
    across = lax.ppermute(mine, "col", exchange)
    settings = jnp.concatenate(
        [
            jnp.stack([core, 0]).astype(jnp.int32),
            sign_table.reshape(-1),
            perm_table.reshape(-1),
        ]
    )
    ops = jnp.tile(insertion_ops, (1, 1, 1, spins))

    result = None
    for index in range(PIECES + 2):
        before = ()
        if index == MINE:
            before = (mine,)
        elif index == COLUMNS:
            came = tie(across, *[chain.outer[-1] for chain in chains])
            chosen = jnp.where((owner // spin_size == side)[:, None, None, None], mine, came)
        elif index == FOLD:
            other = lax.ppermute(chosen, "spin", exchange)
            before = folded = fold(settings, chosen, other, ops)
        elif index in BLOCKS:
            for first in BLOCKS[index]:
                result = block(folded, first, chains, result)
            before = (result,)
        for chain in chains:
            chain.step(index, *before)
    result = block(folded, PIECES - 2 * GROUP, chains, result)
    return block(folded, PIECES - GROUP, chains, result)


def insertion_matrices(insertion_ops, sign_table, perm_table):
    spins = sign_table.shape[1]
    vec_count = insertion_ops.shape[2]
    order = spins * vec_count
    hit = perm_table[:, :, None] == jnp.arange(spins)[None, None, :]
    sign = sign_table[:, :, None]

    def weight(plus, minus):
        value = (sign == plus).astype(jnp.float32) - (sign == minus).astype(jnp.float32)
        return jnp.where(hit, value, 0.0)[:, :, None, :, None]

    real_weight, imag_weight = weight(0, 2), weight(1, 3)
    op_real = insertion_ops[:, 0][:, None, :, None, :]
    op_imag = insertion_ops[:, 1][:, None, :, None, :]
    real = (real_weight * op_real - imag_weight * op_imag).reshape(-1, order, order)
    imag = (real_weight * op_imag + imag_weight * op_real).reshape(-1, order, order)
    return jnp.concatenate(
        [jnp.concatenate([real, imag], axis=2), jnp.concatenate([-imag, real], axis=2)], axis=1
    )


def spread(value, axis, root):
    mine = lax.axis_index(axis) == root
    return lax.psum(jnp.where(mine, value, jnp.zeros_like(value)), axis)


def general(perambulator, insertion_ops, ins_times, sign_table, perm_table):
    vec_count = insertion_ops.shape[2]
    order = sign_table.shape[1] * vec_count
    _, row_count, col_count = perambulator.shape
    piece_rows = min(order, row_count)
    times_local = col_count // order
    gamma = insertion_matrices(insertion_ops, sign_table, perm_table)

    def dot(a, b):
        return jnp.dot(a, b, precision=lax.Precision.HIGHEST)

    real = imag = 0.0
    for k in range(insertion_ops.shape[0]):
        moment = ins_times[k]
        column = spread(
            lax.dynamic_slice_in_dim(perambulator, moment % times_local * order, order, 2),
            ("col", "spin"),
            moment // times_local,
        )
        received = []
        for piece in range(order // piece_rows):
            start = moment * order + piece * piece_rows
            candidate = lax.dynamic_slice_in_dim(perambulator, start % row_count, piece_rows, 1)
            received.append(spread(candidate, "row", start // row_count))
        slab = jnp.concatenate(received, axis=1)
        folded = dot(jnp.concatenate([column[0], column[1]], axis=1), gamma[k])
        left, right = folded[:, :order], folded[:, order:]
        real = real + dot(left, slab[0]) - dot(right, slab[1])
        imag = imag + dot(left, slab[1]) + dot(right, slab[0])
    return jnp.stack([real, imag])


def solution(mesh):
    def shards(perambulator, insertion_ops, ins_times, sign_table, perm_table):
        order = sign_table.shape[1] * insertion_ops.shape[2]
        fits = (
            mesh.shape["row"] == LINE
            and insertion_ops.shape[0] == 2
            and mesh.shape["col"] == 2
            and mesh.shape["spin"] == 2
            and perambulator.shape[1] % order == 0
        )
        arguments = (perambulator, insertion_ops, ins_times, sign_table, perm_table)
        return planned(*arguments) if fits else general(*arguments)

    return jax.shard_map(
        shards,
        mesh=mesh,
        in_specs=(P(None, ("cfg", "row"), ("col", "spin")), P(), P(), P(), P()),
        out_specs=P(None, ("cfg", "row"), ("col", "spin")),
        check_vma=False,
    )
```
